32 devices in a mesh: wide: 16 (over z, y, core), narrow: 2 (over x).
Axes of the slice: x: 2, y: 2, z: 4, core: 2. Of those that a mesh axis runs over, the one named last changes fastest.
Arguments:
- fine_cot: float32 [2, 32, 128, 128], P(None, 'wide', 'narrow'), may hold values from -6 to 6
- obstacle: int32 [2, 32, 128, 128], P(None, 'wide', 'narrow'), may hold values 0 or 1
- sigma: float32 [32, 128, 128], P('wide', 'narrow'), may hold values from 0.2 to 20
Outputs:
- fine_adjoint: float32 [2, 32, 128, 128], P(None, 'wide', 'narrow')
- coarse_adjoint: float32 [16, 2, 16, 64], P('wide', 'narrow')
The draws below stay inside these ranges and needn't reach their ends.
All inputs are finite; a program needn't handle non-finite values. No bound on the sum of `obstacle` on one device may be relied on, other than what follows from the above.
Results may differ from the reference program's by a relative error of at most 0.00011.
Values sent between devices are 32-bit elements; how exact they have to be, the bound alone decides.
A program may use at most 64 MiB of HBM per device.

```python
import math
import jax
import jax.numpy as jnp
from jax import lax

NZ = 128
SWEEPS = 4
DIRS = 2
NX = 32
NY = 128
NXC = 16
NYC = 64
NZC = 16


def place_ends(array, rng, least, top_value):
    place = [jax.random.randint(jax.random.fold_in(rng, axis), (), 0, length) for axis, length in enumerate(array.shape)]
    longest = array.shape.index(max(array.shape))
    beside = place[:longest] + [(place[longest] + 1) % array.shape[longest]] + place[longest + 1:]
    return array.at[tuple(place)].set(least).at[tuple(beside)].set(top_value)


def block_levels(stream_key, extent, shards, least, largest):
    def one(axis_at, shards_of):
        heights = jax.random.uniform(jax.random.fold_in(jax.random.fold_in(stream_key, 6), axis_at), (shards_of,), jnp.float32, least / len(shards), largest / len(shards))
        return jnp.repeat(jnp.exp(heights), extent[axis_at] // shards_of).reshape((-1,) + (1,) * (len(extent) - axis_at - 1))

    level = one(*shards[0])
    for cut in shards[1:]:
        level = level * one(*cut)
    return level


def gaussian(key, dims, width, most, shards=(), kind=jnp.bfloat16):
    loudness = block_levels(key, dims, shards, -0.22, 0.18) if shards else 1.0
    entries = jax.random.normal(key, dims, jnp.float32) * width * loudness
    return jnp.minimum(jnp.maximum(entries, -most), most).astype(kind)


def setup_inputs(seed: int = 0) -> dict:
    splits = jax.random.split(jax.random.key(seed), 4)
    fine_cot = gaussian(splits[0], (DIRS, NX, NY, NZ), 1.0, 6.0, ((1, 16), (2, 2)), jnp.float32)
    obstacle = place_ends((jax.random.randint(splits[1], (DIRS, NX, NY, NZ), 0, 5) < 4).astype(jnp.int32), jax.random.fold_in(splits[1], 1), 0, 1)
    sigma = jnp.clip(jnp.exp(math.log(20.0) - 4.6051702 * jax.random.uniform(splits[2], (NX, NY, NZ), jnp.float32) ** block_levels(splits[2], (NX, NY, NZ), ((0, 16), (1, 2)), -0.2, 0.2)), 0.2, 20.0)
    return {"fine_cot": fine_cot, "obstacle": obstacle, "sigma": sigma}


OMEGA = 0.8
COEF_X = 1.0
COEF_Y = 1.0
COEF_Z = 4.0
SHIFT = 0.02

def sine_table(rows, cols, count):
    product = (rows[:, None] + 1) * (cols[None, :] + 1) % (2 * (count + 1))
    angle = jnp.pi * product.astype(jnp.float32) / (count + 1)
    return jnp.sqrt(2.0 / (count + 1)) * jnp.sin(angle)

def eigen_values(index, count):
    return 2.0 - 2.0 * jnp.cos(jnp.pi * (index + 1).astype(jnp.float32) / (count + 1))

def reference(fine_cot, obstacle, sigma):
    diag = 6.0 + sigma

    def smooth(pair):
        grad, obs = pair
        fluid = obs.astype(jnp.float32)
        for sweep in range(SWEEPS):
            weighted = OMEGA * fluid * grad / diag
            padded = jnp.pad(weighted, 1)
            beside = padded[2:, 1:-1, 1:-1] + padded[:-2, 1:-1, 1:-1]
            beside = beside + padded[1:-1, 2:, 1:-1] + padded[1:-1, :-2, 1:-1]
            beside = beside + padded[1:-1, 1:-1, 2:] + padded[1:-1, 1:-1, :-2]
            grad = grad - diag * weighted + beside
        return grad
    fine_adjoint = lax.map(smooth, (fine_cot, obstacle))
    coarse = fine_adjoint.reshape(DIRS, NXC, 2, NYC, 2, NZC, 8).sum(axis=(2, 4, 6))
    coarse = jnp.transpose(coarse, (1, 0, 3, 2))
    index_x = jnp.arange(NXC, dtype=jnp.int32)
    index_y = jnp.arange(NYC, dtype=jnp.int32)
    index_z = jnp.arange(NZC, dtype=jnp.int32)
    table_x = sine_table(index_x, index_x, NXC)
    table_y = sine_table(index_y, index_y, NYC)
    table_z = sine_table(index_z, index_z, NZC)
    high = lax.Precision.HIGHEST

    def transform(field):
        field = jnp.einsum('xdzy,yv->xdzv', field, table_y, precision=high)
        field = jnp.einsum('xdzv,zw->xdwv', field, table_z, precision=high)
        return jnp.einsum('kx,xdwv->kdwv', table_x, field, precision=high)
    spectrum = transform(coarse)
    denom = COEF_X * eigen_values(index_x, NXC)[:, None, None, None] + COEF_Y * eigen_values(index_y, NYC)[None, None, None, :] + COEF_Z * eigen_values(index_z, NZC)[None, None, :, None] + SHIFT
    scaled = spectrum / denom
    return (fine_adjoint, transform(scaled))
```

```python
import functools

import jax
import jax.numpy as jnp
import numpy as np
from jax import lax
from jax.experimental import pallas as pl
from jax.experimental.pallas import tpu as pltpu
from jax.sharding import PartitionSpec as P

SWEEPS = 4
OMEGA = 0.8
COEF_X = 1.0
COEF_Y = 1.0
COEF_Z = 4.0
SHIFT = 0.02
MESH = pl.DeviceIdType.MESH
LANES = 128


def sine(count):
    index = np.arange(count, dtype=np.int64) + 1
    product = index[:, None] * index[None, :] % (2 * (count + 1))
    return np.sqrt(2.0 / (count + 1)) * np.sin(np.pi * product / (count + 1))


def eigen(count):
    return 2.0 - 2.0 * np.cos(np.pi * (np.arange(count) + 1) / (count + 1))


def tables(dirs, cells_y, cells_z, narrow, coarse_x, coarse_y, coarse_z):
    part = LANES // coarse_y
    rows = coarse_z // part
    s_y, s_z = sine(coarse_y), sine(coarse_z)
    lift = np.repeat(s_z, cells_z // coarse_z, axis=0).T
    fine = np.repeat(s_y, 2, axis=0).reshape(narrow, cells_y, coarse_y)
    spread = np.zeros((narrow, dirs, dirs, cells_y, part, coarse_y))
    for d in range(dirs):
        spread[:, d, d] = fine[:, :, None, :]
    spread = spread.reshape(narrow, dirs, dirs * cells_y, LANES)
    plane = COEF_Y * eigen(coarse_y)[None, :] + COEF_Z * eigen(coarse_z)[:, None] + SHIFT
    plane = plane.reshape(part, rows, coarse_y).transpose(1, 0, 2).reshape(rows, LANES)
    steps = np.arange(2 * coarse_x + 1)
    wave = np.cos(np.pi * (np.outer(steps, np.arange(coarse_x) + 1) % (2 * coarse_x + 2)) / (coarse_x + 1))
    inverse = 1.0 / (COEF_X * eigen(coarse_x)[:, None] + plane.reshape(1, -1))
    green = (wave @ inverse / (coarse_x + 1)).reshape(-1, rows, LANES)
    mix = np.zeros((part * coarse_z, LANES))
    mix[:, :rows] = s_z.reshape(coarse_z, part, rows).transpose(1, 0, 2).reshape(part * coarse_z, rows)
    back = np.zeros((LANES, LANES))
    back[:, :coarse_y] = np.tile(s_y, (part, 1))
    return [np.asarray(t, np.float32) for t in (lift, spread, green, mix, back)]


def dot(a, b, dims=((1,), (0,))):
    return lax.dot_general(
        a, b, (dims, ((), ())), precision=lax.Precision.HIGHEST, preferred_element_type=jnp.float32
    )


def kernel(
    wide, narrow, cot, obs, sig, lift_h, spread_h, green_h, mix_h, back_h, grad, coarse,
    cc, ww, hx, hy, ys, lift, spread, green, mix, back, pack, recv,
    tsem, sx, rx, sy, ry, sc, rc,
):
    dirs, cells_x, cells_y, cells_z = cot.shape
    last = cells_x - 1
    w = lax.axis_index("wide")
    n = lax.axis_index("narrow")
    total = wide * narrow
    me = w * narrow + n

    barrier = pltpu.get_barrier_semaphore()

    def greet(k, carry):
        peer = lax.rem(me + k, total)
        pl.semaphore_signal(
            barrier, inc=1, device_id=(lax.div(peer, narrow), lax.rem(peer, narrow)), device_id_type=MESH
        )
        return carry

    lax.fori_loop(1, total, greet, 0)

    loads = [
        pltpu.make_async_copy(src, dst, tsem.at[i])
        for i, (src, dst) in enumerate(
            ((lift_h, lift), (spread_h.at[n], spread), (green_h, green), (mix_h, mix), (back_h, back))
        )
    ]
    for load in loads:
        load.start()

    edges = (w > 0, w < wide - 1)
    sides = (n > 0, n < narrow - 1)
    for s in range(2):

        @pl.when(jnp.logical_not(edges[s]))
        def _():
            for sweep in range(SWEEPS):
                hx[sweep, s] = jnp.zeros(hx.shape[2:], jnp.float32)

        @pl.when(jnp.logical_not(sides[s]))
        def _():
            for sweep in range(SWEEPS):
                hy[sweep, s] = jnp.zeros(hy.shape[2:], jnp.float32)

    for x in range(cells_x):
        share = OMEGA / (6.0 + sig[x])
        for d in range(dirs):
            fluid = obs[d, x].astype(jnp.float32)
            cc[x, d] = share * fluid
            grad[d, x] = cot[d, x]

    def wide_copy(sweep, s):
        return pltpu.make_async_remote_copy(
            src_ref=ww.at[sweep, 0 if s == 0 else last],
            dst_ref=hx.at[sweep, 1 - s],
            send_sem=sx.at[sweep, s],
            recv_sem=rx.at[sweep, 1 - s],
            device_id=(w - 1 if s == 0 else w + 1, n),
            device_id_type=MESH,
        )

    def wide_arrival(sweep, s):
        return pltpu.make_async_copy(hx.at[sweep, s], hx.at[sweep, s], rx.at[sweep, s])

    def narrow_copy(sweep, s):
        return pltpu.make_async_remote_copy(
            src_ref=ys.at[sweep, s],
            dst_ref=hy.at[sweep, 1 - s],
            send_sem=sy.at[sweep, s],
            recv_sem=ry.at[sweep, 1 - s],
            device_id=(w, n - 1 if s == 0 else n + 1),
            device_id_type=MESH,
        )

    def narrow_arrival(sweep, s):
        return pltpu.make_async_copy(hy.at[sweep, s], hy.at[sweep, s], ry.at[sweep, s])

    lane = lax.broadcasted_iota(jnp.int32, (cells_y, cells_z), 1)
    row = lax.broadcasted_iota(jnp.int32, (cells_y, cells_z), 0)
    for sweep in range(SWEEPS):
        for x in range(cells_x):
            for d in range(dirs):
                value = cc[x, d] * grad[d, x]
                ww[sweep, x, d] = value
                ys[sweep, 0, x * dirs + d] = value[0]
                ys[sweep, 1, x * dirs + d] = value[cells_y - 1]
        if sweep == 0:
            pl.semaphore_wait(barrier, total - 1)
        for s in range(2):

            @pl.when(edges[s])
            def _():
                wide_copy(sweep, s).start()

            @pl.when(sides[s])
            def _():
                narrow_copy(sweep, s).start()

        for x in range(cells_x):
            for d in range(dirs):
                here = ww[sweep, x, d]
                keep = jnp.where(cc[x, d] > 0.0, 1.0 - OMEGA, 1.0)
                near = grad[d, x] * keep
                near += jnp.where(lane == 0, 0.0, pltpu.roll(here, 1, 1))
                near += jnp.where(lane == cells_z - 1, 0.0, pltpu.roll(here, cells_z - 1, 1))
                near += jnp.where(row == 0, 0.0, pltpu.roll(here, 1, 0))
                near += jnp.where(row == cells_y - 1, 0.0, pltpu.roll(here, cells_y - 1, 0))
                if x > 0:
                    near += ww[sweep, x - 1, d]
                if x < last:
                    near += ww[sweep, x + 1, d]
                grad[d, x] = near
        for s in range(2):

            @pl.when(sides[s])
            def _():
                narrow_arrival(sweep, s).wait()

        for x in range(cells_x):
            for d in range(dirs):
                r = x * dirs + d
                grad[d, x, 0:1] += hy[sweep, 0, r : r + 1]
                grad[d, x, cells_y - 1 : cells_y] += hy[sweep, 1, r : r + 1]
        for s in range(2):

            @pl.when(edges[s])
            def _():
                wide_arrival(sweep, s).wait()

            for d in range(dirs):
                grad[d, 0 if s == 0 else last] += hx[sweep, s, d]

    for load in loads:
        load.wait()
    rows = recv.shape[1]
    slab = jnp.concatenate([sum(grad[d, x] for x in range(cells_x)) for d in range(dirs)], axis=0)
    modes = dot(lift[...], slab, ((1,), (1,)))
    part = lift.shape[0] // rows
    width = LANES // part
    column = lax.broadcasted_iota(jnp.int32, (rows, LANES), 1)
    for d in range(dirs):
        wave = dot(modes, spread[d])
        packed = wave[0:rows]
        for h in range(1, part):
            packed = jnp.where(column < h * width, packed, wave[h * rows : (h + 1) * rows])
        pack[d] = packed

    def send(k, carry):
        peer = lax.rem(me + k, total)
        other = lax.rem(peer, narrow)
        for d in range(dirs // narrow):
            pltpu.make_async_remote_copy(
                src_ref=pack.at[other],
                dst_ref=recv.at[me],
                send_sem=sc,
                recv_sem=rc,
                device_id=(lax.div(peer, narrow), other),
                device_id_type=MESH,
            ).start()
        return carry

    lax.fori_loop(1, total, send, 0)
    recv[me] = pack[n]
    all_but_one = recv.at[pl.ds(0, total - 1)]
    pltpu.make_async_copy(all_but_one, all_but_one, rc).wait()

    def solve(x, carry):
        near = green[lax.abs(w - x)] - green[w + x + 2]
        field = recv[x * narrow]
        for m in range(1, narrow):
            field += recv[x * narrow + m]
        return carry + near * field

    solved = lax.fori_loop(0, wide, solve, jnp.zeros((rows, LANES), jnp.float32), unroll=min(wide, 16))
    wave = dot(mix[:, 0:rows], solved)
    count_z = coarse.shape[2]
    column = lax.broadcasted_iota(jnp.int32, (count_z, LANES), 1)
    both = wave[0:count_z]
    for h in range(1, part):
        both = jnp.where(column < h * width, both, wave[h * count_z : (h + 1) * count_z])
    coarse[0, 0] = dot(both, back[...])[:, 0 : coarse.shape[3]]

    for sweep in range(SWEEPS):
        for s in range(2):

            @pl.when(edges[s])
            def _():
                wide_copy(sweep, s).wait_send()

            @pl.when(sides[s])
            def _():
                narrow_copy(sweep, s).wait_send()

    pltpu.make_async_copy(all_but_one, all_but_one, sc).wait()


def body(wide, narrow, fine_cot, obstacle, sigma):
    dirs, cells_x, cells_y, cells_z = fine_cot.shape
    coarse_x, coarse_y, coarse_z = wide * cells_x // 2, narrow * cells_y // 2, cells_z // 8
    made = tables(dirs, cells_y, cells_z, narrow, coarse_x, coarse_y, coarse_z)
    lift, spread, green, mix, back = made
    total = wide * narrow
    rows = green.shape[1]
    f32 = jnp.float32
    vmem = pl.BlockSpec(memory_space=pltpu.VMEM)
    anywhere = pl.BlockSpec(memory_space=pl.ANY)
    plane = (cells_y, cells_z)
    return pl.pallas_call(
        functools.partial(kernel, wide, narrow),
        out_shape=(
            jax.ShapeDtypeStruct(fine_cot.shape, f32),
            jax.ShapeDtypeStruct((1, 1, coarse_z, coarse_y), f32),
        ),
        in_specs=[vmem] * 3 + [anywhere] * 5,
        out_specs=(vmem, vmem),
        scratch_shapes=[
            pltpu.VMEM((cells_x, dirs) + plane, f32),
            pltpu.VMEM((SWEEPS, cells_x, dirs) + plane, f32),
            pltpu.VMEM((SWEEPS, 2, dirs) + plane, f32),
            pltpu.VMEM((SWEEPS, 2, cells_x * dirs, cells_z), f32),
            pltpu.VMEM((SWEEPS, 2, cells_x * dirs, cells_z), f32),
            pltpu.VMEM(lift.shape, f32),
            pltpu.VMEM(spread.shape[1:], f32),
            pltpu.VMEM(green.shape, f32),
            pltpu.VMEM(mix.shape, f32),
            pltpu.VMEM(back.shape, f32),
            pltpu.VMEM((dirs, rows, LANES), f32),
            pltpu.VMEM((total, rows, LANES), f32),
            pltpu.SemaphoreType.DMA((5,)),
            pltpu.SemaphoreType.DMA((SWEEPS, 2)),
            pltpu.SemaphoreType.DMA((SWEEPS, 2)),
            pltpu.SemaphoreType.DMA((SWEEPS, 2)),
            pltpu.SemaphoreType.DMA((SWEEPS, 2)),
            pltpu.SemaphoreType.DMA,
            pltpu.SemaphoreType.DMA,
        ],
        compiler_params=pltpu.CompilerParams(
            collective_id=0, has_side_effects=True, vmem_limit_bytes=40 * 2**20
        ),
    )(fine_cot, obstacle, sigma, *made)


def solution(mesh):
    placed = (
        P(None, "wide", "narrow", None),
        P(None, "wide", "narrow", None),
        P("wide", "narrow", None),
    )
    return jax.shard_map(
        functools.partial(body, mesh.shape["wide"], mesh.shape["narrow"]),
        mesh=mesh,
        in_specs=placed,
        out_specs=(P(None, "wide", "narrow", None), P("wide", "narrow", None, None)),
        check_vma=False,
    )
```

```python
import functools

import jax
import jax.numpy as jnp
import numpy as np
from jax import lax
from jax.experimental import pallas as pl
from jax.experimental.pallas import tpu as pltpu
from jax.sharding import PartitionSpec as P

SWEEPS = 4
OMEGA = 0.8
COEF_X = 1.0
COEF_Y = 1.0
COEF_Z = 4.0
SHIFT = 0.02
MESH = pl.DeviceIdType.MESH
LANES = 128


def sine(count):
    index = np.arange(count, dtype=np.int64) + 1
    product = index[:, None] * index[None, :] % (2 * (count + 1))
    return np.sqrt(2.0 / (count + 1)) * np.sin(np.pi * product / (count + 1))


def eigen(count):
    return 2.0 - 2.0 * np.cos(np.pi * (np.arange(count) + 1) / (count + 1))


def tables(dirs, cells_y, cells_z, narrow, coarse_x, coarse_y, coarse_z):
    part = LANES // coarse_y
    rows = coarse_z // part
    s_y, s_z = sine(coarse_y), sine(coarse_z)
    lift = np.repeat(s_z, cells_z // coarse_z, axis=0).T
    fine = np.repeat(s_y, 2, axis=0).reshape(narrow, cells_y, coarse_y)
    spread = np.zeros((narrow, dirs, dirs, cells_y, part, coarse_y))
    for d in range(dirs):
        spread[:, d, d] = fine[:, :, None, :]
    spread = spread.reshape(narrow, dirs, dirs * cells_y, LANES)
    plane = COEF_Y * eigen(coarse_y)[None, :] + COEF_Z * eigen(coarse_z)[:, None] + SHIFT
    plane = plane.reshape(part, rows, coarse_y).transpose(1, 0, 2).reshape(rows, LANES)
    steps = np.arange(2 * coarse_x + 1)
    wave = np.cos(np.pi * (np.outer(steps, np.arange(coarse_x) + 1) % (2 * coarse_x + 2)) / (coarse_x + 1))
    inverse = 1.0 / (COEF_X * eigen(coarse_x)[:, None] + plane.reshape(1, -1))
    green = (wave @ inverse / (coarse_x + 1)).reshape(-1, rows, LANES)
    mix = np.zeros((part * coarse_z, LANES))
    mix[:, :rows] = s_z.reshape(coarse_z, part, rows).transpose(1, 0, 2).reshape(part * coarse_z, rows)
    back = np.zeros((LANES, LANES))
    back[:, :coarse_y] = np.tile(s_y, (part, 1))
    return [np.asarray(t, np.float32) for t in (lift, spread, green, mix, back)]


def dot(a, b, dims=((1,), (0,))):
    return lax.dot_general(
        a, b, (dims, ((), ())), precision=lax.Precision.HIGHEST, preferred_element_type=jnp.float32
    )


def kernel(
    wide, narrow, cot_h, obs_h, sig_h, lift_h, spread_h, green_h, mix_h, back_h, grad, coarse,
    obs, sig, cc, ww, hx, hy, ys, lift, spread, green, mix, back, pack, recv,
    tsem, sx, rx, sy, ry, sc, rc,
):
    dirs, cells_x, cells_y, cells_z = grad.shape
    last = cells_x - 1
    w = lax.axis_index("wide")
    n = lax.axis_index("narrow")
    total = wide * narrow
    me = w * narrow + n

    loads = [
        pltpu.make_async_copy(src, dst, tsem.at[i])
        for i, (src, dst) in enumerate(
            (
                (sig_h, sig),
                (obs_h, obs),
                (cot_h, grad),
                (lift_h, lift),
                (spread_h.at[n], spread),
                (green_h, green),
                (mix_h, mix),
                (back_h, back),
            )
        )
    ]
    for load in loads:
        load.start()

    barrier = pltpu.get_barrier_semaphore()

    def greet(k, carry):
        peer = lax.rem(me + k, total)
        pl.semaphore_signal(
            barrier, inc=1, device_id=(lax.div(peer, narrow), lax.rem(peer, narrow)), device_id_type=MESH
        )
        return carry

    lax.fori_loop(1, total, greet, 0)

    edges = (w > 0, w < wide - 1)
    sides = (n > 0, n < narrow - 1)
    for s in range(2):

        @pl.when(jnp.logical_not(edges[s]))
        def _():
            for sweep in range(SWEEPS):
                hx[sweep, s] = jnp.zeros(hx.shape[2:], jnp.float32)

        @pl.when(jnp.logical_not(sides[s]))
        def _():
            for sweep in range(SWEEPS):
                hy[sweep, s] = jnp.zeros(hy.shape[2:], jnp.float32)

    for load in loads[:3]:
        load.wait()
    for x in range(cells_x):
        share = OMEGA / (6.0 + sig[x])
        for d in range(dirs):
            fluid = obs[d, x].astype(jnp.float32)
            cc[x, d] = share * fluid

    def wide_copy(sweep, s):
        return pltpu.make_async_remote_copy(
            src_ref=ww.at[sweep, 0 if s == 0 else last],
            dst_ref=hx.at[sweep, 1 - s],
            send_sem=sx.at[sweep, s],
            recv_sem=rx.at[sweep, 1 - s],
            device_id=(w - 1 if s == 0 else w + 1, n),
            device_id_type=MESH,
        )

    def wide_arrival(sweep, s):
        return pltpu.make_async_copy(hx.at[sweep, s], hx.at[sweep, s], rx.at[sweep, s])

    def narrow_copy(sweep, s):
        return pltpu.make_async_remote_copy(
            src_ref=ys.at[sweep, s],
            dst_ref=hy.at[sweep, 1 - s],
            send_sem=sy.at[sweep, s],
            recv_sem=ry.at[sweep, 1 - s],
            device_id=(w, n - 1 if s == 0 else n + 1),
            device_id_type=MESH,
        )

    def narrow_arrival(sweep, s):
        return pltpu.make_async_copy(hy.at[sweep, s], hy.at[sweep, s], ry.at[sweep, s])

    lane = lax.broadcasted_iota(jnp.int32, (cells_y, cells_z), 1)
    row = lax.broadcasted_iota(jnp.int32, (cells_y, cells_z), 0)
    for sweep in range(SWEEPS):
        for x in range(cells_x):
            for d in range(dirs):
                value = cc[x, d] * grad[d, x]
                ww[sweep, x, d] = value
                ys[sweep, 0, x * dirs + d] = value[0]
                ys[sweep, 1, x * dirs + d] = value[cells_y - 1]
        if sweep == 0:
            pl.semaphore_wait(barrier, total - 1)
        for s in range(2):

            @pl.when(edges[s])
            def _():
                wide_copy(sweep, s).start()

            @pl.when(sides[s])
            def _():
                narrow_copy(sweep, s).start()

        for x in range(cells_x):
            for d in range(dirs):
                here = ww[sweep, x, d]
                keep = jnp.where(cc[x, d] > 0.0, 1.0 - OMEGA, 1.0)
                near = grad[d, x] * keep
                near += jnp.where(lane == 0, 0.0, pltpu.roll(here, 1, 1))
                near += jnp.where(lane == cells_z - 1, 0.0, pltpu.roll(here, cells_z - 1, 1))
                near += jnp.where(row == 0, 0.0, pltpu.roll(here, 1, 0))
                near += jnp.where(row == cells_y - 1, 0.0, pltpu.roll(here, cells_y - 1, 0))
                if x > 0:
                    near += ww[sweep, x - 1, d]
                if x < last:
                    near += ww[sweep, x + 1, d]
                grad[d, x] = near
        for s in range(2):

            @pl.when(sides[s])
            def _():
                narrow_arrival(sweep, s).wait()

        for x in range(cells_x):
            for d in range(dirs):
                r = x * dirs + d
                grad[d, x, 0:1] += hy[sweep, 0, r : r + 1]
                grad[d, x, cells_y - 1 : cells_y] += hy[sweep, 1, r : r + 1]
        for s in range(2):

            @pl.when(edges[s])
            def _():
                wide_arrival(sweep, s).wait()

            for d in range(dirs):
                grad[d, 0 if s == 0 else last] += hx[sweep, s, d]

    for load in loads[3:]:
        load.wait()
    rows = recv.shape[1]
    slab = jnp.concatenate([sum(grad[d, x] for x in range(cells_x)) for d in range(dirs)], axis=0)
    modes = dot(lift[...], slab, ((1,), (1,)))
    part = lift.shape[0] // rows
    width = LANES // part
    column = lax.broadcasted_iota(jnp.int32, (rows, LANES), 1)
    for d in range(dirs):
        wave = dot(modes, spread[d])
        packed = wave[0:rows]
        for h in range(1, part):
            packed = jnp.where(column < h * width, packed, wave[h * rows : (h + 1) * rows])
        pack[d] = packed

    def send(k, carry):
        peer = lax.rem(me + k, total)
        other = lax.rem(peer, narrow)
        for d in range(dirs // narrow):
            pltpu.make_async_remote_copy(
                src_ref=pack.at[other],
                dst_ref=recv.at[me],
                send_sem=sc,
                recv_sem=rc,
                device_id=(lax.div(peer, narrow), other),
                device_id_type=MESH,
            ).start()
        return carry

    lax.fori_loop(1, total, send, 0)
    recv[me] = pack[n]
    all_but_one = recv.at[pl.ds(0, total - 1)]
    pltpu.make_async_copy(all_but_one, all_but_one, rc).wait()

    def solve(x, carry):
        near = green[lax.abs(w - x)] - green[w + x + 2]
        field = recv[x * narrow]
        for m in range(1, narrow):
            field += recv[x * narrow + m]
        return carry + near * field

    solved = lax.fori_loop(0, wide, solve, jnp.zeros((rows, LANES), jnp.float32), unroll=min(wide, 16))
    wave = dot(mix[:, 0:rows], solved)
    count_z = coarse.shape[2]
    column = lax.broadcasted_iota(jnp.int32, (count_z, LANES), 1)
    both = wave[0:count_z]
    for h in range(1, part):
        both = jnp.where(column < h * width, both, wave[h * count_z : (h + 1) * count_z])
    coarse[0, 0] = dot(both, back[...])[:, 0 : coarse.shape[3]]

    for sweep in range(SWEEPS):
        for s in range(2):

            @pl.when(edges[s])
            def _():
                wide_copy(sweep, s).wait_send()

            @pl.when(sides[s])
            def _():
                narrow_copy(sweep, s).wait_send()

    pltpu.make_async_copy(all_but_one, all_but_one, sc).wait()


def body(wide, narrow, fine_cot, obstacle, sigma):
    dirs, cells_x, cells_y, cells_z = fine_cot.shape
    coarse_x, coarse_y, coarse_z = wide * cells_x // 2, narrow * cells_y // 2, cells_z // 8
    made = tables(dirs, cells_y, cells_z, narrow, coarse_x, coarse_y, coarse_z)
    lift, spread, green, mix, back = made
    total = wide * narrow
    rows = green.shape[1]
    f32 = jnp.float32
    vmem = pl.BlockSpec(memory_space=pltpu.VMEM)
    stay = pl.BlockSpec(memory_space=pl.ANY)
    plane = (cells_y, cells_z)
    return pl.pallas_call(
        functools.partial(kernel, wide, narrow),
        out_shape=(
            jax.ShapeDtypeStruct(fine_cot.shape, f32),
            jax.ShapeDtypeStruct((1, 1, coarse_z, coarse_y), f32),
        ),
        in_specs=[stay] * 8,
        out_specs=(vmem, vmem),
        scratch_shapes=[
            pltpu.VMEM(obstacle.shape, obstacle.dtype),
            pltpu.VMEM(sigma.shape, f32),
            pltpu.VMEM((cells_x, dirs) + plane, f32),
            pltpu.VMEM((SWEEPS, cells_x, dirs) + plane, f32),
            pltpu.VMEM((SWEEPS, 2, dirs) + plane, f32),
            pltpu.VMEM((SWEEPS, 2, cells_x * dirs, cells_z), f32),
            pltpu.VMEM((SWEEPS, 2, cells_x * dirs, cells_z), f32),
            pltpu.VMEM(lift.shape, f32),
            pltpu.VMEM(spread.shape[1:], f32),
            pltpu.VMEM(green.shape, f32),
            pltpu.VMEM(mix.shape, f32),
            pltpu.VMEM(back.shape, f32),
            pltpu.VMEM((dirs, rows, LANES), f32),
            pltpu.VMEM((total, rows, LANES), f32),
            pltpu.SemaphoreType.DMA((8,)),
            pltpu.SemaphoreType.DMA((SWEEPS, 2)),
            pltpu.SemaphoreType.DMA((SWEEPS, 2)),
            pltpu.SemaphoreType.DMA((SWEEPS, 2)),
            pltpu.SemaphoreType.DMA((SWEEPS, 2)),
            pltpu.SemaphoreType.DMA,
            pltpu.SemaphoreType.DMA,
        ],
        compiler_params=pltpu.CompilerParams(
            collective_id=0, has_side_effects=True, vmem_limit_bytes=60 * 2**20
        ),
    )(fine_cot, obstacle, sigma, *made)


def solution(mesh):
    placed = (
        P(None, "wide", "narrow", None),
        P(None, "wide", "narrow", None),
        P("wide", "narrow", None),
    )
    return jax.shard_map(
        functools.partial(body, mesh.shape["wide"], mesh.shape["narrow"]),
        mesh=mesh,
        in_specs=placed,
        out_specs=(P(None, "wide", "narrow", None), P("wide", "narrow", None, None)),
        check_vma=False,
    )
```

```python
import functools

import jax
import jax.numpy as jnp
import numpy as np
from jax import lax
from jax.experimental import pallas as pl
from jax.experimental.pallas import tpu as pltpu
from jax.sharding import PartitionSpec as P

SWEEPS = 4
BLOCKS = SWEEPS // 2
OMEGA = 0.8
COEF_X = 1.0
COEF_Y = 1.0
COEF_Z = 4.0
SHIFT = 0.02
MESH = pl.DeviceIdType.MESH
LANES = 128


def sine(count):
    index = np.arange(count, dtype=np.int64) + 1
    product = index[:, None] * index[None, :] % (2 * (count + 1))
    return np.sqrt(2.0 / (count + 1)) * np.sin(np.pi * product / (count + 1))


def eigen(count):
    return 2.0 - 2.0 * np.cos(np.pi * (np.arange(count) + 1) / (count + 1))


def tables(dirs, cells_y, cells_z, narrow, coarse_x, coarse_y, coarse_z):
    part = LANES // coarse_y
    rows = coarse_z // part
    s_y, s_z = sine(coarse_y), sine(coarse_z)
    lift = np.repeat(s_z, cells_z // coarse_z, axis=0).T
    fine = np.repeat(s_y, 2, axis=0).reshape(narrow, cells_y, coarse_y)
    spread = np.zeros((narrow, dirs, dirs, cells_y, part, coarse_y))
    for d in range(dirs):
        spread[:, d, d] = fine[:, :, None, :]
    spread = spread.reshape(narrow, dirs, dirs * cells_y, LANES)
    plane = COEF_Y * eigen(coarse_y)[None, :] + COEF_Z * eigen(coarse_z)[:, None] + SHIFT
    plane = plane.reshape(part, rows, coarse_y).transpose(1, 0, 2).reshape(rows, LANES)
    steps = np.arange(2 * coarse_x + 1)
    wave = np.cos(np.pi * (np.outer(steps, np.arange(coarse_x) + 1) % (2 * coarse_x + 2)) / (coarse_x + 1))
    inverse = 1.0 / (COEF_X * eigen(coarse_x)[:, None] + plane.reshape(1, -1))
    green = (wave @ inverse / (coarse_x + 1)).reshape(-1, rows, LANES)
    mix = np.zeros((part * coarse_z, LANES))
    mix[:, :rows] = s_z.reshape(coarse_z, part, rows).transpose(1, 0, 2).reshape(part * coarse_z, rows)
    back = np.zeros((LANES, LANES))
    back[:, :coarse_y] = np.tile(s_y, (part, 1))
    return [np.asarray(t, np.float32) for t in (lift, spread, green, mix, back)]


def dot(a, b, dims=((1,), (0,))):
    return lax.dot_general(
        a, b, (dims, ((), ())), precision=lax.Precision.HIGHEST, preferred_element_type=jnp.float32
    )


def kernel(
    wide, narrow, cot_h, obs_h, sig_h, lift_h, spread_h, green_h, mix_h, back_h, grad, coarse,
    obs, sig, cc, ww, wl, hx, hc, hy, ys, hk, ks, ax, ay, lift, spread, green, mix, back, pack, recv,
    tsem, sx, rx, sy, ry, sk, rk, sf, rf, sc, rc,
):
    dirs, cells_x, cells_y, cells_z = grad.shape
    last = cells_x - 1
    w = lax.axis_index("wide")
    n = lax.axis_index("narrow")
    total = wide * narrow
    me = w * narrow + n

    loads = [
        pltpu.make_async_copy(src, dst, tsem.at[i])
        for i, (src, dst) in enumerate(
            (
                (sig_h, sig),
                (obs_h, obs),
                (cot_h, grad),
                (lift_h, lift),
                (spread_h.at[n], spread),
                (green_h, green),
                (mix_h, mix),
                (back_h, back),
            )
        )
    ]
    for load in loads:
        load.start()

    barrier = pltpu.get_barrier_semaphore()

    def greet(k, carry):
        peer = lax.rem(me + k, total)
        pl.semaphore_signal(
            barrier, inc=1, device_id=(lax.div(peer, narrow), lax.rem(peer, narrow)), device_id_type=MESH
        )
        return carry

    lax.fori_loop(1, total, greet, 0)

    edges = (w > 0, w < wide - 1)
    sides = (n > 0, n < narrow - 1)
    for s in range(2):

        @pl.when(jnp.logical_not(edges[s]))
        def _():
            hc[s] = jnp.zeros(hc.shape[1:], jnp.float32)
            for block in range(BLOCKS):
                hx[block, s] = jnp.zeros(hx.shape[2:], jnp.float32)

        @pl.when(jnp.logical_not(sides[s]))
        def _():
            for block in range(BLOCKS):
                hy[block, s] = jnp.zeros(hy.shape[2:], jnp.float32)

        for t in range(2):

            @pl.when(jnp.logical_not(edges[s] & sides[t]))
            def _():
                for block in range(BLOCKS):
                    hk[block, s, t] = jnp.zeros(hk.shape[3:], jnp.float32)

    ends = (0, last)
    rims = (0, cells_y - 1)
    for load in loads[:3]:
        load.wait()
    for x in range(cells_x):
        share = OMEGA / (6.0 + sig[x])
        for d in range(dirs):
            cc[x, d] = share * obs[d, x].astype(jnp.float32)

    def beyond(s):
        return w - 1 if s == 0 else w + 1

    def across(t):
        return n - 1 if t == 0 else n + 1

    def remote(src, dst, sent, came, to):
        return pltpu.make_async_remote_copy(
            src_ref=src, dst_ref=dst, send_sem=sent, recv_sem=came, device_id=to, device_id_type=MESH
        )

    def copies(block):
        made = []
        for s in range(2):
            made.append((
                edges[s],
                remote(ww.at[block], hx.at[block, 1 - s], sx.at[block, s], rx.at[block, 1 - s], (beyond(s), n)),
                hx.at[block, s], rx.at[block, s],
            ))
        for t in range(2):
            made.append((
                sides[t],
                remote(ys.at[block, t], hy.at[block, 1 - t], sy.at[block, t], ry.at[block, 1 - t], (w, across(t))),
                hy.at[block, t], ry.at[block, t],
            ))
        for s in range(2):
            for t in range(2):
                made.append((
                    edges[s] & sides[t],
                    remote(
                        ks.at[block, s, t], hk.at[block, 1 - s, 1 - t], sk.at[block, s, t],
                        rk.at[block, 1 - s, 1 - t], (beyond(s), across(t)),
                    ),
                    hk.at[block, s, t], rk.at[block, s, t],
                ))
        if block == 0:
            for s in range(2):
                made.append((
                    edges[s],
                    remote(cc.at[ends[s]], hc.at[1 - s], sf.at[s], rf.at[1 - s], (beyond(s), n)),
                    hc.at[s], rf.at[s],
                ))
        return made

    lane = lax.broadcasted_iota(jnp.int32, (cells_y, cells_z), 1)
    row = lax.broadcasted_iota(jnp.int32, (cells_y, cells_z), 0)

    def along_z(here):
        index = lax.broadcasted_iota(jnp.int32, here.shape, 1)
        return jnp.where(index == 0, 0.0, pltpu.roll(here, 1, 1)) + jnp.where(
            index == cells_z - 1, 0.0, pltpu.roll(here, cells_z - 1, 1)
        )

    def along_y(here, low, high):
        return jnp.where(row == 0, low, pltpu.roll(here, 1, 0)) + jnp.where(
            row == cells_y - 1, high, pltpu.roll(here, cells_y - 1, 0)
        )

    def inner(src):
        for x in range(cells_x):
            for d in range(dirs):
                here = src[x, d]
                keep = jnp.where(cc[x, d] > 0.0, 1.0 - OMEGA, 1.0)
                near = grad[d, x] * keep + along_z(here) + along_y(here, 0.0, 0.0)
                if x > 0:
                    near += src[x - 1, d]
                if x < last:
                    near += src[x + 1, d]
                grad[d, x] = near

    def outer(wide_side, narrow_side):
        for x in range(cells_x):
            for d in range(dirs):
                r = x * dirs + d
                for t in range(2):
                    edge = pl.ds(rims[t], 1)
                    grad[d, x, edge] += narrow_side[t, pl.ds(r, 1)]
        for s in range(2):
            for d in range(dirs):
                grad[d, ends[s]] += wide_side[s, d]

    planes = cells_x * dirs
    for block in range(BLOCKS):
        for x in range(cells_x):
            for d in range(dirs):
                value = cc[x, d] * grad[d, x]
                ww[block, x, d] = value
                r = x * dirs + d
                for t in range(2):
                    step = 1 if t == 0 else -1
                    ys[block, t, 0, r] = value[rims[t]]
                    ys[block, t, 1, r] = value[rims[t] + step]
                    ys[block, t, 2, r] = cc[x, d, rims[t]]
                    for s in range(2):
                        if x == ends[s]:
                            ks[block, s, t, d] = value[rims[t]]
        if block == 0:
            pl.semaphore_wait(barrier, total - 1)
        made = copies(block)
        for there, copy, _, _ in made:
            pl.when(there)(copy.start)
        inner(ww.at[block])
        for there, _, buffer, came in made:
            pl.when(there)(pltpu.make_async_copy(buffer, buffer, came).wait)

        for s in range(2):
            first = 1 - s
            for d in range(dirs):
                here = hx[block, s, ends[first], d]
                around = hx[block, s, ends[first] - (1 if s == 0 else -1), d] + ww[block, ends[s], d]
                around += along_z(here) + along_y(here, hk[block, s, 0, pl.ds(d, 1)], hk[block, s, 1, pl.ds(d, 1)])
                ax[s, d] = (1.0 - OMEGA) * here + hc[s, d] * around
        for t in range(2):
            here = hy[block, t, 0]
            left = jnp.concatenate([hk[block, 0, t], here[: planes - dirs]], axis=0)
            right = jnp.concatenate([here[dirs:], hk[block, 1, t]], axis=0)
            around = hy[block, t, 1] + ys[block, t, 0] + left + right + along_z(here)
            ay[t] = (1.0 - OMEGA) * here + hy[block, t, 2] * around
        for x in range(cells_x):
            for d in range(dirs):
                r = x * dirs + d
                for t in range(2):
                    grad[d, x, pl.ds(rims[t], 1)] += hy[block, t, 0, pl.ds(r, 1)]
        for s in range(2):
            for d in range(dirs):
                grad[d, ends[s]] += hx[block, s, ends[1 - s], d]
        for x in range(cells_x):
            for d in range(dirs):
                wl[x, d] = cc[x, d] * grad[d, x]
        inner(wl)
        outer(ax, ay)

    for load in loads[3:]:
        load.wait()
    rows = recv.shape[1]
    slab = jnp.concatenate([sum(grad[d, x] for x in range(cells_x)) for d in range(dirs)], axis=0)
    modes = dot(lift[...], slab, ((1,), (1,)))
    part = lift.shape[0] // rows
    width = LANES // part
    column = lax.broadcasted_iota(jnp.int32, (rows, LANES), 1)
    for d in range(dirs):
        wave = dot(modes, spread[d])
        packed = wave[0:rows]
        for h in range(1, part):
            packed = jnp.where(column < h * width, packed, wave[h * rows : (h + 1) * rows])
        pack[d] = packed

    def send(k, carry):
        peer = lax.rem(me + k, total)
        other = lax.rem(peer, narrow)
        for d in range(dirs // narrow):
            pltpu.make_async_remote_copy(
                src_ref=pack.at[other],
                dst_ref=recv.at[me],
                send_sem=sc,
                recv_sem=rc,
                device_id=(lax.div(peer, narrow), other),
                device_id_type=MESH,
            ).start()
        return carry

    lax.fori_loop(1, total, send, 0)
    recv[me] = pack[n]
    all_but_one = recv.at[pl.ds(0, total - 1)]
    pltpu.make_async_copy(all_but_one, all_but_one, rc).wait()

    def solve(x, carry):
        near = green[lax.abs(w - x)] - green[w + x + 2]
        field = recv[x * narrow]
        for m in range(1, narrow):
            field += recv[x * narrow + m]
        return carry + near * field

    solved = lax.fori_loop(0, wide, solve, jnp.zeros((rows, LANES), jnp.float32), unroll=min(wide, 16))
    wave = dot(mix[:, 0:rows], solved)
    count_z = coarse.shape[2]
    column = lax.broadcasted_iota(jnp.int32, (count_z, LANES), 1)
    both = wave[0:count_z]
    for h in range(1, part):
        both = jnp.where(column < h * width, both, wave[h * count_z : (h + 1) * count_z])
    coarse[0, 0] = dot(both, back[...])[:, 0 : coarse.shape[3]]

    for block in range(BLOCKS):
        for there, copy, _, _ in copies(block):
            pl.when(there)(copy.wait_send)

    pltpu.make_async_copy(all_but_one, all_but_one, sc).wait()


def body(wide, narrow, fine_cot, obstacle, sigma):
    dirs, cells_x, cells_y, cells_z = fine_cot.shape
    coarse_x, coarse_y, coarse_z = wide * cells_x // 2, narrow * cells_y // 2, cells_z // 8
    made = tables(dirs, cells_y, cells_z, narrow, coarse_x, coarse_y, coarse_z)
    lift, spread, green, mix, back = made
    total = wide * narrow
    rows = green.shape[1]
    f32 = jnp.float32
    vmem = pl.BlockSpec(memory_space=pltpu.VMEM)
    stay = pl.BlockSpec(memory_space=pl.ANY)
    plane = (cells_y, cells_z)
    return pl.pallas_call(
        functools.partial(kernel, wide, narrow),
        out_shape=(
            jax.ShapeDtypeStruct(fine_cot.shape, f32),
            jax.ShapeDtypeStruct((1, 1, coarse_z, coarse_y), f32),
        ),
        in_specs=[stay] * 8,
        out_specs=(vmem, vmem),
        scratch_shapes=[
            pltpu.VMEM(obstacle.shape, obstacle.dtype),
            pltpu.VMEM(sigma.shape, f32),
            pltpu.VMEM((cells_x, dirs) + plane, f32),
            pltpu.VMEM((BLOCKS, cells_x, dirs) + plane, f32),
            pltpu.VMEM((cells_x, dirs) + plane, f32),
            pltpu.VMEM((BLOCKS, 2, cells_x, dirs) + plane, f32),
            pltpu.VMEM((2, dirs) + plane, f32),
            pltpu.VMEM((BLOCKS, 2, 3, cells_x * dirs, cells_z), f32),
            pltpu.VMEM((BLOCKS, 2, 3, cells_x * dirs, cells_z), f32),
            pltpu.VMEM((BLOCKS, 2, 2, dirs, cells_z), f32),
            pltpu.VMEM((BLOCKS, 2, 2, dirs, cells_z), f32),
            pltpu.VMEM((2, dirs) + plane, f32),
            pltpu.VMEM((2, cells_x * dirs, cells_z), f32),
            pltpu.VMEM(lift.shape, f32),
            pltpu.VMEM(spread.shape[1:], f32),
            pltpu.VMEM(green.shape, f32),
            pltpu.VMEM(mix.shape, f32),
            pltpu.VMEM(back.shape, f32),
            pltpu.VMEM((dirs, rows, LANES), f32),
            pltpu.VMEM((total, rows, LANES), f32),
            pltpu.SemaphoreType.DMA((8,)),
            *[pltpu.SemaphoreType.DMA((BLOCKS, 2))] * 4,
            *[pltpu.SemaphoreType.DMA((BLOCKS, 2, 2))] * 2,
            *[pltpu.SemaphoreType.DMA((2,))] * 2,
            pltpu.SemaphoreType.DMA,
            pltpu.SemaphoreType.DMA,
        ],
        compiler_params=pltpu.CompilerParams(
            collective_id=0, has_side_effects=True, vmem_limit_bytes=60 * 2**20
        ),
    )(fine_cot, obstacle, sigma, *made)


def solution(mesh):
    placed = (
        P(None, "wide", "narrow", None),
        P(None, "wide", "narrow", None),
        P("wide", "narrow", None),
    )
    return jax.shard_map(
        functools.partial(body, mesh.shape["wide"], mesh.shape["narrow"]),
        mesh=mesh,
        in_specs=placed,
        out_specs=(P(None, "wide", "narrow", None), P("wide", "narrow", None, None)),
        check_vma=False,
    )
```

```python
import functools

import jax
import jax.numpy as jnp
import numpy as np
from jax import lax
from jax.experimental import pallas as pl
from jax.experimental.pallas import tpu as pltpu
from jax.sharding import PartitionSpec as P

SWEEPS = 4
BLOCKS = SWEEPS // 2
OMEGA = 0.8
COEF_X = 1.0
COEF_Y = 1.0
COEF_Z = 4.0
SHIFT = 0.02
MESH = pl.DeviceIdType.MESH
LANES = 128


def sine(count):
    index = np.arange(count, dtype=np.int64) + 1
    product = index[:, None] * index[None, :] % (2 * (count + 1))
    return np.sqrt(2.0 / (count + 1)) * np.sin(np.pi * product / (count + 1))


def eigen(count):
    return 2.0 - 2.0 * np.cos(np.pi * (np.arange(count) + 1) / (count + 1))


def tables(cells_y, cells_z, narrow, coarse_x, coarse_y, coarse_z):
    part = LANES // coarse_y
    rows = coarse_z // part
    s_y, s_z = sine(coarse_y), sine(coarse_z)
    lift = np.repeat(s_z, cells_z // coarse_z, axis=0).T
    fine = np.repeat(s_y, 2, axis=0).reshape(narrow, cells_y, coarse_y)
    spread = np.tile(fine, (1, 1, part))
    plane = COEF_Y * eigen(coarse_y)[None, :] + COEF_Z * eigen(coarse_z)[:, None] + SHIFT
    plane = plane.reshape(part, rows, coarse_y).transpose(1, 0, 2).reshape(rows, LANES)
    steps = np.arange(2 * coarse_x + 1)
    wave = np.cos(np.pi * (np.outer(steps, np.arange(coarse_x) + 1) % (2 * coarse_x + 2)) / (coarse_x + 1))
    inverse = 1.0 / (COEF_X * eigen(coarse_x)[:, None] + plane.reshape(1, -1))
    green = (wave @ inverse / (coarse_x + 1)).reshape(-1, rows, LANES)
    mix = np.zeros((part * coarse_z, LANES))
    mix[:, :rows] = s_z.reshape(coarse_z, part, rows).transpose(1, 0, 2).reshape(part * coarse_z, rows)
    back = np.zeros((LANES, LANES))
    back[:, :coarse_y] = np.tile(s_y, (part, 1))
    return [np.asarray(t, np.float32) for t in (lift, spread, green, mix, back)]


def dot(a, b, dims=((1,), (0,))):
    return lax.dot_general(
        a, b, (dims, ((), ())), precision=lax.Precision.HIGHEST, preferred_element_type=jnp.float32
    )


def kernel(
    wide, narrow, cot_h, obs_h, sig_h, lift_h, spread_h, green_h, mix_h, back_h, grad_h, coarse,
    grad, obs, sig, cc, ww, wl, hx, hc, hy, ys, hk, ks, ax, ay, lift, spread, green, mix, back, pack, recv,
    tsem, sx, rx, sy, ry, sk, rk, sf, rf, osem, sc, rc,
):
    dirs, cells_x, cells_y, cells_z = grad.shape
    last = cells_x - 1
    w = lax.axis_index("wide")
    n = lax.axis_index("narrow")
    total = wide * narrow
    me = w * narrow + n

    loads = [
        pltpu.make_async_copy(src, dst, tsem.at[i])
        for i, (src, dst) in enumerate(
            (
                (sig_h, sig),
                (obs_h, obs),
                (cot_h, grad),
                (lift_h, lift),
                (spread_h.at[n], spread),
                (green_h, green),
                (mix_h, mix),
                (back_h, back),
            )
        )
    ]
    for load in loads:
        load.start()

    barrier = pltpu.get_barrier_semaphore()

    def greet(k, carry):
        peer = lax.rem(me + k, total)
        pl.semaphore_signal(
            barrier, inc=1, device_id=(lax.div(peer, narrow), lax.rem(peer, narrow)), device_id_type=MESH
        )
        return carry

    lax.fori_loop(1, total, greet, 0)

    edges = (w > 0, w < wide - 1)
    sides = (n > 0, n < narrow - 1)
    for s in range(2):

        @pl.when(jnp.logical_not(edges[s]))
        def _():
            hc[s] = jnp.zeros(hc.shape[1:], jnp.float32)
            for block in range(BLOCKS):
                hx[block, s] = jnp.zeros(hx.shape[2:], jnp.float32)

        @pl.when(jnp.logical_not(sides[s]))
        def _():
            for block in range(BLOCKS):
                hy[block, s] = jnp.zeros(hy.shape[2:], jnp.float32)

        for t in range(2):

            @pl.when(jnp.logical_not(edges[s] & sides[t]))
            def _():
                for block in range(BLOCKS):
                    hk[block, s, t] = jnp.zeros(hk.shape[3:], jnp.float32)

    ends = (0, last)
    rims = (0, cells_y - 1)
    for load in loads[:3]:
        load.wait()
    for x in range(cells_x):
        share = OMEGA / (6.0 + sig[x])
        for d in range(dirs):
            cc[x, d] = share * obs[d, x].astype(jnp.float32)

    def beyond(s):
        return w - 1 if s == 0 else w + 1

    def across(t):
        return n - 1 if t == 0 else n + 1

    def remote(src, dst, sent, came, to):
        return pltpu.make_async_remote_copy(
            src_ref=src, dst_ref=dst, send_sem=sent, recv_sem=came, device_id=to, device_id_type=MESH
        )

    def copies(block, d):
        made = []
        for s in range(2):
            made.append((
                edges[s],
                remote(
                    ww.at[block, :, d], hx.at[block, 1 - s, :, d], sx.at[block, s, d], rx.at[block, 1 - s, d],
                    (beyond(s), n),
                ),
                hx.at[block, s, :, d], rx.at[block, s, d],
            ))
        for t in range(2):
            made.append((
                sides[t],
                remote(
                    ys.at[block, t, d], hy.at[block, 1 - t, d], sy.at[block, t, d], ry.at[block, 1 - t, d],
                    (w, across(t)),
                ),
                hy.at[block, t, d], ry.at[block, t, d],
            ))
        for s in range(2):
            for t in range(2):
                made.append((
                    edges[s] & sides[t],
                    remote(
                        ks.at[block, s, t, d], hk.at[block, 1 - s, 1 - t, d], sk.at[block, s, t, d],
                        rk.at[block, 1 - s, 1 - t, d], (beyond(s), across(t)),
                    ),
                    hk.at[block, s, t, d], rk.at[block, s, t, d],
                ))
        if block == 0:
            for s in range(2):
                made.append((
                    edges[s],
                    remote(cc.at[ends[s], d], hc.at[1 - s, d], sf.at[s, d], rf.at[1 - s, d], (beyond(s), n)),
                    hc.at[s, d], rf.at[s, d],
                ))
        return made

    lane = lax.broadcasted_iota(jnp.int32, (cells_y, cells_z), 1)
    row = lax.broadcasted_iota(jnp.int32, (cells_y, cells_z), 0)

    def along_z(here):
        index = lax.broadcasted_iota(jnp.int32, here.shape, 1)
        return jnp.where(index == 0, 0.0, pltpu.roll(here, 1, 1)) + jnp.where(
            index == cells_z - 1, 0.0, pltpu.roll(here, cells_z - 1, 1)
        )

    def along_y(here, low, high):
        return jnp.where(row == 0, low, pltpu.roll(here, 1, 0)) + jnp.where(
            row == cells_y - 1, high, pltpu.roll(here, cells_y - 1, 0)
        )

    def inner(src, d):
        for x in range(cells_x):
            here = src[x, d]
            keep = jnp.where(cc[x, d] > 0.0, 1.0 - OMEGA, 1.0)
            near = grad[d, x] * keep + along_z(here) + along_y(here, 0.0, 0.0)
            if x > 0:
                near += src[x - 1, d]
            if x < last:
                near += src[x + 1, d]
            grad[d, x] = near

    def begin(block, d):
        for x in range(cells_x):
            value = cc[x, d] * grad[d, x]
            ww[block, x, d] = value
            for t in range(2):
                step = 1 if t == 0 else -1
                ys[block, t, d, 0, x] = value[rims[t]]
                ys[block, t, d, 1, x] = value[rims[t] + step]
                ys[block, t, d, 2, x] = cc[x, d, rims[t]]
                for s in range(2):
                    if x == ends[s]:
                        ks[block, s, t, d, 0] = value[rims[t]]

    def launch(block, d):
        for there, copy, _, _ in copies(block, d):
            pl.when(there)(copy.start)

    def finish(block, d):
        for there, _, buffer, came in copies(block, d):
            pl.when(there)(pltpu.make_async_copy(buffer, buffer, came).wait)
        for s in range(2):
            near_at = ends[1 - s]
            far_at = near_at - (1 if s == 0 else -1)
            here = hx[block, s, near_at, d]
            around = hx[block, s, far_at, d] + ww[block, ends[s], d]
            around += along_z(here) + along_y(here, hk[block, s, 0, d], hk[block, s, 1, d])
            ax[s, d] = (1.0 - OMEGA) * here + hc[s, d] * around
            grad[d, ends[s]] += here
        for t in range(2):
            here = hy[block, t, d, 0]
            left = jnp.concatenate([hk[block, 0, t, d], here[: cells_x - 1]], axis=0)
            right = jnp.concatenate([here[1:], hk[block, 1, t, d]], axis=0)
            around = hy[block, t, d, 1] + ys[block, t, d, 0] + left + right + along_z(here)
            ay[t, d] = (1.0 - OMEGA) * here + hy[block, t, d, 2] * around
            for x in range(cells_x):
                grad[d, x, pl.ds(rims[t], 1)] += hy[block, t, d, 0, pl.ds(x, 1)]
        for x in range(cells_x):
            wl[x, d] = cc[x, d] * grad[d, x]
        inner(wl, d)
        for t in range(2):
            for x in range(cells_x):
                grad[d, x, pl.ds(rims[t], 1)] += ay[t, d, pl.ds(x, 1)]
        for s in range(2):
            grad[d, ends[s]] += ax[s, d]

    rows = recv.shape[1]
    part = lift.shape[0] // rows
    width = LANES // part
    column = lax.broadcasted_iota(jnp.int32, (rows, LANES), 1)

    def give(d):
        slab = sum(grad[d, x] for x in range(cells_x))
        wave = dot(dot(lift[...], slab, ((1,), (1,))), spread[...])
        packed = wave[0:rows]
        for h in range(1, part):
            packed = jnp.where(column < h * width, packed, wave[h * rows : (h + 1) * rows])
        pack[d] = packed
        owner = d // (dirs // narrow)

        def send(k, carry):
            pltpu.make_async_remote_copy(
                src_ref=pack.at[d],
                dst_ref=recv.at[me],
                send_sem=sc,
                recv_sem=rc,
                device_id=(lax.rem(w + k, wide), owner),
                device_id_type=MESH,
            ).start()
            return carry

        lax.fori_loop(1, wide, send, 0)

        @pl.when(n != owner)
        def _():
            send(0, 0)

        @pl.when(n == owner)
        def _():
            recv[me] = packed

    for d in range(dirs):
        begin(0, d)
        if d == 0:
            pl.semaphore_wait(barrier, total - 1)
        launch(0, d)
    for d in range(dirs):
        inner(ww.at[0], d)
    for load in loads[3:]:
        load.wait()
    stores = []
    for block in range(BLOCKS):
        for d in range(dirs):
            finish(block, d)
            if block + 1 < BLOCKS:
                begin(block + 1, d)
                launch(block + 1, d)
                inner(ww.at[block + 1], d)
            else:
                give(d)
                stores.append(pltpu.make_async_copy(grad.at[d], grad_h.at[d], osem.at[d]))
                stores[-1].start()

    all_but_one = recv.at[pl.ds(0, total - 1)]
    pltpu.make_async_copy(all_but_one, all_but_one, rc).wait()

    def solve(x, carry):
        near = green[lax.abs(w - x)] - green[w + x + 2]
        field = recv[x * narrow]
        for m in range(1, narrow):
            field += recv[x * narrow + m]
        return carry + near * field

    solved = lax.fori_loop(0, wide, solve, jnp.zeros((rows, LANES), jnp.float32), unroll=min(wide, 16))
    wave = dot(mix[:, 0:rows], solved)
    count_z = coarse.shape[2]
    column = lax.broadcasted_iota(jnp.int32, (count_z, LANES), 1)
    both = wave[0:count_z]
    for h in range(1, part):
        both = jnp.where(column < h * width, both, wave[h * count_z : (h + 1) * count_z])
    coarse[0, 0] = dot(both, back[...])[:, 0 : coarse.shape[3]]

    for block in range(BLOCKS):
        for d in range(dirs):
            for there, copy, _, _ in copies(block, d):
                pl.when(there)(copy.wait_send)
    for store in stores:
        store.wait()

    pltpu.make_async_copy(all_but_one, all_but_one, sc).wait()


def body(wide, narrow, fine_cot, obstacle, sigma):
    dirs, cells_x, cells_y, cells_z = fine_cot.shape
    coarse_x, coarse_y, coarse_z = wide * cells_x // 2, narrow * cells_y // 2, cells_z // 8
    made = tables(cells_y, cells_z, narrow, coarse_x, coarse_y, coarse_z)
    lift, spread, green, mix, back = made
    total = wide * narrow
    rows = green.shape[1]
    f32 = jnp.float32
    vmem = pl.BlockSpec(memory_space=pltpu.VMEM)
    stay = pl.BlockSpec(memory_space=pl.ANY)
    plane = (cells_y, cells_z)
    return pl.pallas_call(
        functools.partial(kernel, wide, narrow),
        out_shape=(
            jax.ShapeDtypeStruct(fine_cot.shape, f32),
            jax.ShapeDtypeStruct((1, 1, coarse_z, coarse_y), f32),
        ),
        in_specs=[stay] * 8,
        out_specs=(stay, vmem),
        scratch_shapes=[
            pltpu.VMEM(fine_cot.shape, f32),
            pltpu.VMEM(obstacle.shape, obstacle.dtype),
            pltpu.VMEM(sigma.shape, f32),
            pltpu.VMEM((cells_x, dirs) + plane, f32),
            pltpu.VMEM((BLOCKS, cells_x, dirs) + plane, f32),
            pltpu.VMEM((cells_x, dirs) + plane, f32),
            pltpu.VMEM((BLOCKS, 2, cells_x, dirs) + plane, f32),
            pltpu.VMEM((2, dirs) + plane, f32),
            pltpu.VMEM((BLOCKS, 2, dirs, 3, cells_x, cells_z), f32),
            pltpu.VMEM((BLOCKS, 2, dirs, 3, cells_x, cells_z), f32),
            pltpu.VMEM((BLOCKS, 2, 2, dirs, 1, cells_z), f32),
            pltpu.VMEM((BLOCKS, 2, 2, dirs, 1, cells_z), f32),
            pltpu.VMEM((2, dirs) + plane, f32),
            pltpu.VMEM((2, dirs, cells_x, cells_z), f32),
            pltpu.VMEM(lift.shape, f32),
            pltpu.VMEM(spread.shape[1:], f32),
            pltpu.VMEM(green.shape, f32),
            pltpu.VMEM(mix.shape, f32),
            pltpu.VMEM(back.shape, f32),
            pltpu.VMEM((dirs, rows, LANES), f32),
            pltpu.VMEM((total, rows, LANES), f32),
            pltpu.SemaphoreType.DMA((8,)),
            *[pltpu.SemaphoreType.DMA((BLOCKS, 2, dirs))] * 4,
            *[pltpu.SemaphoreType.DMA((BLOCKS, 2, 2, dirs))] * 2,
            *[pltpu.SemaphoreType.DMA((2, dirs))] * 2,
            pltpu.SemaphoreType.DMA((dirs,)),
            pltpu.SemaphoreType.DMA,
            pltpu.SemaphoreType.DMA,
        ],
        compiler_params=pltpu.CompilerParams(
            collective_id=0, has_side_effects=True, vmem_limit_bytes=60 * 2**20
        ),
    )(fine_cot, obstacle, sigma, *made)


def solution(mesh):
    placed = (
        P(None, "wide", "narrow", None),
        P(None, "wide", "narrow", None),
        P("wide", "narrow", None),
    )
    return jax.shard_map(
        functools.partial(body, mesh.shape["wide"], mesh.shape["narrow"]),
        mesh=mesh,
        in_specs=placed,
        out_specs=(P(None, "wide", "narrow", None), P("wide", "narrow", None, None)),
        check_vma=False,
    )
```

```python
import functools

import jax
import jax.numpy as jnp
import numpy as np
from jax import lax
from jax.experimental import pallas as pl
from jax.experimental.pallas import tpu as pltpu
from jax.sharding import PartitionSpec as P

SWEEPS = 4
BLOCKS = SWEEPS // 2
OMEGA = 0.8
COEF_X = 1.0
COEF_Y = 1.0
COEF_Z = 4.0
SHIFT = 0.02
MESH = pl.DeviceIdType.MESH
LANES = 128


def sine(count):
    index = np.arange(count, dtype=np.int64) + 1
    product = index[:, None] * index[None, :] % (2 * (count + 1))
    return np.sqrt(2.0 / (count + 1)) * np.sin(np.pi * product / (count + 1))


def eigen(count):
    return 2.0 - 2.0 * np.cos(np.pi * (np.arange(count) + 1) / (count + 1))


def tables(cells_y, cells_z, narrow, coarse_x, coarse_y, coarse_z):
    part = LANES // coarse_y
    rows = coarse_z // part
    s_y, s_z = sine(coarse_y), sine(coarse_z)
    lift = np.repeat(s_z, cells_z // coarse_z, axis=0).T
    fine = np.repeat(s_y, 2, axis=0).reshape(narrow, cells_y, coarse_y)
    spread = np.tile(fine, (1, 1, part))
    plane = COEF_Y * eigen(coarse_y)[None, :] + COEF_Z * eigen(coarse_z)[:, None] + SHIFT
    plane = plane.reshape(part, rows, coarse_y).transpose(1, 0, 2).reshape(rows, LANES)
    steps = np.arange(2 * coarse_x + 1)
    wave = np.cos(np.pi * (np.outer(steps, np.arange(coarse_x) + 1) % (2 * coarse_x + 2)) / (coarse_x + 1))
    inverse = 1.0 / (COEF_X * eigen(coarse_x)[:, None] + plane.reshape(1, -1))
    green = (wave @ inverse / (coarse_x + 1)).reshape(-1, rows, LANES)
    mix = np.zeros((part * coarse_z, LANES))
    mix[:, :rows] = s_z.reshape(coarse_z, part, rows).transpose(1, 0, 2).reshape(part * coarse_z, rows)
    back = np.zeros((LANES, LANES))
    back[:, :coarse_y] = np.tile(s_y, (part, 1))
    return [np.asarray(t, np.float32) for t in (lift, spread, green, mix, back)]


def dot(a, b, dims=((1,), (0,))):
    return lax.dot_general(
        a, b, (dims, ((), ())), precision=lax.Precision.HIGHEST, preferred_element_type=jnp.float32
    )


def kernel(
    wide, narrow, cot_h, obs_h, sig_h, table_h, grad_h, coarse,
    grad, obs, sig, cc, ww, wl, hx, hc, hy, ys, hk, ks, ax, ay, lift, spread, green, mix, back, pack, recv,
    tsem, sx, rx, sy, ry, sk, rk, sf, rf, osem, sc, rc,
):
    dirs, cells_x, cells_y, cells_z = grad.shape
    last = cells_x - 1
    w = lax.axis_index("wide")
    n = lax.axis_index("narrow")
    total = wide * narrow
    me = w * narrow + n

    starts = np.cumsum([0, lift.shape[0], narrow * cells_y, green.shape[0], mix.shape[0]]).tolist()

    def rows_of(i, dst):
        first = starts[i] + (pl.multiple_of(n * cells_y, 8) if i == 1 else 0)
        return table_h.at[pl.ds(first, dst.shape[0])], dst

    loads = [
        pltpu.make_async_copy(src, dst, tsem.at[i])
        for i, (src, dst) in enumerate(
            (
                (sig_h, sig),
                (obs_h, obs),
                (cot_h, grad),
                rows_of(0, lift),
                rows_of(1, spread),
                rows_of(2, green),
                rows_of(3, mix),
                rows_of(4, back),
            )
        )
    ]
    for load in loads:
        load.start()

    barrier = pltpu.get_barrier_semaphore()

    def greet(k, carry):
        peer = lax.rem(me + k, total)
        pl.semaphore_signal(
            barrier, inc=1, device_id=(lax.div(peer, narrow), lax.rem(peer, narrow)), device_id_type=MESH
        )
        return carry

    lax.fori_loop(1, total, greet, 0)

    edges = (w > 0, w < wide - 1)
    sides = (n > 0, n < narrow - 1)
    for s in range(2):

        @pl.when(jnp.logical_not(edges[s]))
        def _():
            hc[s] = jnp.zeros(hc.shape[1:], jnp.float32)
            for block in range(BLOCKS):
                hx[block, s] = jnp.zeros(hx.shape[2:], jnp.float32)

        @pl.when(jnp.logical_not(sides[s]))
        def _():
            for block in range(BLOCKS):
                hy[block, s] = jnp.zeros(hy.shape[2:], jnp.float32)

        for t in range(2):

            @pl.when(jnp.logical_not(edges[s] & sides[t]))
            def _():
                for block in range(BLOCKS):
                    hk[block, s, t] = jnp.zeros(hk.shape[3:], jnp.float32)

    ends = (0, last)
    rims = (0, cells_y - 1)
    for load in loads[:3]:
        load.wait()
    for x in range(cells_x):
        share = OMEGA / (6.0 + sig[x])
        for d in range(dirs):
            cc[x, d] = share * obs[d, x].astype(jnp.float32)

    def beyond(s):
        return w - 1 if s == 0 else w + 1

    def across(t):
        return n - 1 if t == 0 else n + 1

    def remote(src, dst, sent, came, to):
        return pltpu.make_async_remote_copy(
            src_ref=src, dst_ref=dst, send_sem=sent, recv_sem=came, device_id=to, device_id_type=MESH
        )

    def copies(block, d):
        made = []
        for s in range(2):
            made.append((
                edges[s],
                remote(
                    ww.at[block, :, d], hx.at[block, 1 - s, :, d], sx.at[block, s, d], rx.at[block, 1 - s, d],
                    (beyond(s), n),
                ),
                hx.at[block, s, :, d], rx.at[block, s, d],
            ))
        for t in range(2):
            made.append((
                sides[t],
                remote(
                    ys.at[block, t, d], hy.at[block, 1 - t, d], sy.at[block, t, d], ry.at[block, 1 - t, d],
                    (w, across(t)),
                ),
                hy.at[block, t, d], ry.at[block, t, d],
            ))
        for s in range(2):
            for t in range(2):
                made.append((
                    edges[s] & sides[t],
                    remote(
                        ks.at[block, s, t, d], hk.at[block, 1 - s, 1 - t, d], sk.at[block, s, t, d],
                        rk.at[block, 1 - s, 1 - t, d], (beyond(s), across(t)),
                    ),
                    hk.at[block, s, t, d], rk.at[block, s, t, d],
                ))
        if block == 0:
            for s in range(2):
                made.append((
                    edges[s],
                    remote(cc.at[ends[s], d], hc.at[1 - s, d], sf.at[s, d], rf.at[1 - s, d], (beyond(s), n)),
                    hc.at[s, d], rf.at[s, d],
                ))
        return made

    lane = lax.broadcasted_iota(jnp.int32, (cells_y, cells_z), 1)
    row = lax.broadcasted_iota(jnp.int32, (cells_y, cells_z), 0)

    def along_z(here):
        index = lax.broadcasted_iota(jnp.int32, here.shape, 1)
        return jnp.where(index == 0, 0.0, pltpu.roll(here, 1, 1)) + jnp.where(
            index == cells_z - 1, 0.0, pltpu.roll(here, cells_z - 1, 1)
        )

    def along_y(here, low, high):
        return jnp.where(row == 0, low, pltpu.roll(here, 1, 0)) + jnp.where(
            row == cells_y - 1, high, pltpu.roll(here, cells_y - 1, 0)
        )

    def inner(src, d):
        for x in range(cells_x):
            here = src[x, d]
            keep = jnp.where(cc[x, d] > 0.0, 1.0 - OMEGA, 1.0)
            near = grad[d, x] * keep + along_z(here) + along_y(here, 0.0, 0.0)
            if x > 0:
                near += src[x - 1, d]
            if x < last:
                near += src[x + 1, d]
            grad[d, x] = near

    def begin(block, d):
        for x in range(cells_x):
            value = cc[x, d] * grad[d, x]
            ww[block, x, d] = value
            for t in range(2):
                step = 1 if t == 0 else -1
                ys[block, t, d, 0, x] = value[rims[t]]
                ys[block, t, d, 1, x] = value[rims[t] + step]
                ys[block, t, d, 2, x] = cc[x, d, rims[t]]
                for s in range(2):
                    if x == ends[s]:
                        ks[block, s, t, d, 0] = value[rims[t]]

    def launch(block, d):
        made = copies(block, d)
        for there, copy, _, _ in made[2:8] + made[:2] + made[8:]:
            pl.when(there)(copy.start)

    def finish(block, d):
        for there, _, buffer, came in copies(block, d):
            pl.when(there)(pltpu.make_async_copy(buffer, buffer, came).wait)
        for s in range(2):
            near_at = ends[1 - s]
            far_at = near_at - (1 if s == 0 else -1)
            here = hx[block, s, near_at, d]
            around = hx[block, s, far_at, d] + ww[block, ends[s], d]
            around += along_z(here) + along_y(here, hk[block, s, 0, d], hk[block, s, 1, d])
            ax[s, d] = (1.0 - OMEGA) * here + hc[s, d] * around
            grad[d, ends[s]] += here
        for t in range(2):
            here = hy[block, t, d, 0]
            left = jnp.concatenate([hk[block, 0, t, d], here[: cells_x - 1]], axis=0)
            right = jnp.concatenate([here[1:], hk[block, 1, t, d]], axis=0)
            around = hy[block, t, d, 1] + ys[block, t, d, 0] + left + right + along_z(here)
            ay[t, d] = (1.0 - OMEGA) * here + hy[block, t, d, 2] * around
            for x in range(cells_x):
                grad[d, x, pl.ds(rims[t], 1)] += hy[block, t, d, 0, pl.ds(x, 1)]
        for x in range(cells_x):
            wl[x, d] = cc[x, d] * grad[d, x]
        inner(wl, d)
        for t in range(2):
            for x in range(cells_x):
                grad[d, x, pl.ds(rims[t], 1)] += ay[t, d, pl.ds(x, 1)]
        for s in range(2):
            grad[d, ends[s]] += ax[s, d]

    rows = recv.shape[1]
    part = lift.shape[0] // rows
    width = LANES // part
    column = lax.broadcasted_iota(jnp.int32, (rows, LANES), 1)

    def give(d):
        slab = sum(grad[d, x] for x in range(cells_x))
        wave = dot(dot(lift[...], slab, ((1,), (1,))), spread[...])
        packed = wave[0:rows]
        for h in range(1, part):
            packed = jnp.where(column < h * width, packed, wave[h * rows : (h + 1) * rows])
        pack[d] = packed
        owner = d // (dirs // narrow)

        def send(k, carry):
            pltpu.make_async_remote_copy(
                src_ref=pack.at[d],
                dst_ref=recv.at[me],
                send_sem=sc,
                recv_sem=rc,
                device_id=(lax.rem(w + k, wide), owner),
                device_id_type=MESH,
            ).start()
            return carry

        lax.fori_loop(1, wide, send, 0)

        @pl.when(n != owner)
        def _():
            send(0, 0)

        @pl.when(n == owner)
        def _():
            recv[me] = packed

    for d in range(dirs):
        begin(0, d)
        if d == 0:
            pl.semaphore_wait(barrier, total - 1)
        launch(0, d)
    for d in range(dirs):
        inner(ww.at[0], d)
    for load in loads[3:]:
        load.wait()
    stores = []
    for block in range(BLOCKS):
        for d in range(dirs):
            finish(block, d)
            if block + 1 < BLOCKS:
                begin(block + 1, d)
                launch(block + 1, d)
                inner(ww.at[block + 1], d)
            else:
                give(d)
                stores.append(pltpu.make_async_copy(grad.at[d], grad_h.at[d], osem.at[d]))
                stores[-1].start()

    all_but_one = recv.at[pl.ds(0, total - 1)]
    pltpu.make_async_copy(all_but_one, all_but_one, rc).wait()

    def solve(x, carry):
        near = green[pl.ds(pl.multiple_of(lax.abs(w - x) * rows, 8), rows)]
        near -= green[pl.ds(pl.multiple_of((w + x + 2) * rows, 8), rows)]
        field = recv[x * narrow]
        for m in range(1, narrow):
            field += recv[x * narrow + m]
        return carry + near * field

    solved = lax.fori_loop(0, wide, solve, jnp.zeros((rows, LANES), jnp.float32), unroll=min(wide, 16))
    wave = dot(mix[:, 0:rows], solved)
    count_z = coarse.shape[2]
    column = lax.broadcasted_iota(jnp.int32, (count_z, LANES), 1)
    both = wave[0:count_z]
    for h in range(1, part):
        both = jnp.where(column < h * width, both, wave[h * count_z : (h + 1) * count_z])
    coarse[0, 0] = dot(both, back[...])[:, 0 : coarse.shape[3]]

    for block in range(BLOCKS):
        for d in range(dirs):
            for there, copy, _, _ in copies(block, d):
                pl.when(there)(copy.wait_send)
    for store in stores:
        store.wait()

    pltpu.make_async_copy(all_but_one, all_but_one, sc).wait()


def body(wide, narrow, fine_cot, obstacle, sigma):
    dirs, cells_x, cells_y, cells_z = fine_cot.shape
    coarse_x, coarse_y, coarse_z = wide * cells_x // 2, narrow * cells_y // 2, cells_z // 8
    made = tables(cells_y, cells_z, narrow, coarse_x, coarse_y, coarse_z)
    lift, spread, green, mix, back = made
    total = wide * narrow
    rows = green.shape[1]
    green = green.reshape(-1, LANES)
    table = np.concatenate([lift, spread.reshape(-1, LANES), green, mix, back], axis=0)
    f32 = jnp.float32
    vmem = pl.BlockSpec(memory_space=pltpu.VMEM)
    stay = pl.BlockSpec(memory_space=pl.ANY)
    plane = (cells_y, cells_z)
    return pl.pallas_call(
        functools.partial(kernel, wide, narrow),
        out_shape=(
            jax.ShapeDtypeStruct(fine_cot.shape, f32),
            jax.ShapeDtypeStruct((1, 1, coarse_z, coarse_y), f32),
        ),
        in_specs=[stay] * 4,
        out_specs=(stay, vmem),
        scratch_shapes=[
            pltpu.VMEM(fine_cot.shape, f32),
            pltpu.VMEM(obstacle.shape, obstacle.dtype),
            pltpu.VMEM(sigma.shape, f32),
            pltpu.VMEM((cells_x, dirs) + plane, f32),
            pltpu.VMEM((BLOCKS, cells_x, dirs) + plane, f32),
            pltpu.VMEM((cells_x, dirs) + plane, f32),
            pltpu.VMEM((BLOCKS, 2, cells_x, dirs) + plane, f32),
            pltpu.VMEM((2, dirs) + plane, f32),
            pltpu.VMEM((BLOCKS, 2, dirs, 3, cells_x, cells_z), f32),
            pltpu.VMEM((BLOCKS, 2, dirs, 3, cells_x, cells_z), f32),
            pltpu.VMEM((BLOCKS, 2, 2, dirs, 1, cells_z), f32),
            pltpu.VMEM((BLOCKS, 2, 2, dirs, 1, cells_z), f32),
            pltpu.VMEM((2, dirs) + plane, f32),
            pltpu.VMEM((2, dirs, cells_x, cells_z), f32),
            pltpu.VMEM(lift.shape, f32),
            pltpu.VMEM(spread.shape[1:], f32),
            pltpu.VMEM(green.shape, f32),
            pltpu.VMEM(mix.shape, f32),
            pltpu.VMEM(back.shape, f32),
            pltpu.VMEM((dirs, rows, LANES), f32),
            pltpu.VMEM((total, rows, LANES), f32),
            pltpu.SemaphoreType.DMA((8,)),
            *[pltpu.SemaphoreType.DMA((BLOCKS, 2, dirs))] * 4,
            *[pltpu.SemaphoreType.DMA((BLOCKS, 2, 2, dirs))] * 2,
            *[pltpu.SemaphoreType.DMA((2, dirs))] * 2,
            pltpu.SemaphoreType.DMA((dirs,)),
            pltpu.SemaphoreType.DMA,
            pltpu.SemaphoreType.DMA,
        ],
        compiler_params=pltpu.CompilerParams(
            collective_id=0, has_side_effects=True, vmem_limit_bytes=55050 * 2**10
        ),
    )(fine_cot, obstacle, sigma, table)


def solution(mesh):
    placed = (
        P(None, "wide", "narrow", None),
        P(None, "wide", "narrow", None),
        P("wide", "narrow", None),
    )
    return jax.shard_map(
        functools.partial(body, mesh.shape["wide"], mesh.shape["narrow"]),
        mesh=mesh,
        in_specs=placed,
        out_specs=(P(None, "wide", "narrow", None), P("wide", "narrow", None, None)),
        check_vma=False,
    )
```
